256 devices in a mesh: expert: 64 (over z, x, core), help: 4 (over y).
Axes of the slice: x: 4, y: 4, z: 8, core: 2. Of those that a mesh axis runs over, the one named last changes fastest.
Arguments:
- activations: bfloat16 [65536, 8, 1024], P(('expert', 'help')), may hold values from -60 to 60
- routes: int32 [65536, 8], P(('expert', 'help')), may hold values from 0 to 255, all different within a row; in each aligned block of 256 rows (0 to 255, 256 to 511, ...) at most 16 rows name the same one
- owner_map: int32 [256], replicated, may hold values from 0 to 255, each once
- damp_pct: int32 [256], P(('expert', 'help')), may hold values from 5 to 20
- scale_code: int32 [256, 3584], P(('expert', 'help')), may hold values from 8 to 32
- weight_panel: bfloat16 [256, 128, 3584], P(('expert', 'help')), may hold values from -4 to 4
Outputs:
- quantized: float32 [256, 128, 3584], P(('expert', 'help'))
- factor_strip: float32 [256, 128, 1024], P(('expert', 'help'))
The draws below stay inside these ranges and needn't reach their ends.
Inputs may be any that keep to these rules, and one draw needn't show every extreme that they name: `routes`: each token names 8 distinct experts. Among the 256 tokens of one device no expert is named more than 16 times, and some device reaches 16. `owner_map`: each owner slot is named by exactly one expert.
All inputs are finite; a program needn't handle non-finite values.
Results may differ from the reference program's by a relative error of at most 0.0003.
Values may be sent and summed in bfloat16 or wider, within the bound.
No kernel may reach another device: no remote copies, remote signals or barrier semaphores. Data moves between devices by JAX's collectives and lax.ppermute only.
A program may use at most 128 MiB of HBM per device.

```python
import math
import jax
import jax.numpy as jnp
import numpy as np
from jax import lax

FF = 1024
D_OUT = 3584
TOP = 8
PANEL = 128
TOK_DEV = 256
EXPERTS = 256
TOKENS = 65536
CAP = 16
N_EXPERT = 64
N_HELP = 4


def draw_activations(key, part):
    key = jax.random.fold_in(key, 11)
    key_values, key_rows, key_cols = jax.random.split(key, 3)
    row_scale = jnp.exp(jax.random.uniform(key_rows, (TOKENS, TOP, 1), jnp.float32, math.log(0.5), math.log(5.0)))
    col_scale = jnp.exp(jax.random.uniform(key_cols, (1, 1, FF), jnp.float32, math.log(0.3), math.log(3.0)))
    summed = jnp.zeros((TOKENS, TOP, FF), jnp.float32)
    power_sum = 0.0
    for scale_level in range(FF.bit_length()):
        block_width = 2 ** scale_level
        if FF % block_width == 0:
            amplitude = 2.0 ** (-0.3 * scale_level)
            level_key = jax.random.fold_in(key_values, scale_level)
            coarse_shape = (TOKENS, TOP, FF // block_width, 1)
            coarse = jax.random.truncated_normal(level_key, -4.0, 4.0, coarse_shape, jnp.float32)
            spread = jnp.broadcast_to(coarse, (TOKENS, TOP, FF // block_width, block_width)).reshape(TOKENS, TOP, FF)
            summed = summed + amplitude * spread
            power_sum = power_sum + amplitude * amplitude
    values = summed / math.sqrt(power_sum)
    return jnp.clip(values * row_scale * col_scale, -60.0, 60.0).astype(jnp.bfloat16)


def with_ends(array, stream_key, low, largest):
    longest = array.shape.index(max(array.shape))
    spots = []
    for shift in (0, 1):
        where = [jax.random.randint(jax.random.fold_in(stream_key, axis), (), 0, length) for axis, length in enumerate(array.shape)]
        where[longest] = (where[longest] + shift) % array.shape[longest]
        spots.append(tuple(where))
    return array.at[spots[0]].set(low).at[spots[1]].set(largest)


def block_levels(own_key, extent, cuts, least, high):
    loudness, own = 1.0, jax.random.fold_in(own_key, 6)
    for position, shards_of in cuts:
        steps = jnp.exp(jax.random.uniform(jax.random.fold_in(own, position), (shards_of,), jnp.float32, least / len(cuts), high / len(cuts)))
        loudness = loudness * jnp.repeat(steps, extent[position] // shards_of).reshape([-1 if axis == position else 1 for axis in range(len(extent))])
    return loudness


def shared_out(key, own, number, rows, number_of, top, limit, skew):
    sequence = jax.random.permutation(key, number_of)
    heavy_load, common = portions_of(number_of, rows * top, limit, skew, True), portions_of(number_of, rows * top, limit, skew, False)
    places = jnp.arange(number_of)

    def named(sizes, rotation):
        used = int((sizes > 0).sum())
        fixed = max(1, used // 4)
        passed = fixed + (places - fixed + rotation * (used - fixed)) % max(1, number_of - fixed)
        return jnp.zeros((number_of,), jnp.int32).at[sequence[jnp.where(places < fixed, places, passed)]].set(jnp.asarray(sizes, jnp.int32))

    sizes = jnp.where(number % 4 == 0, named(heavy_load, number // 4), named(common, number - number // 4 - 1))
    mixed = jax.random.permutation(jax.random.fold_in(own, 3), number_of)
    donor, receiver = mixed[0:number_of // 2 * 2:2], mixed[1:number_of // 2 * 2:2]
    room = jnp.minimum(sizes[donor] - 1, limit - sizes[receiver]) // 2
    room = jnp.where((donor == sequence[0]) | (receiver == sequence[0]) | (sizes[receiver] == 0), 0, jnp.maximum(room, 0))
    passed = jax.random.randint(jax.random.fold_in(own, 4), (number_of // 2,), 0, 1 << 20) % (room + 1)
    sizes = sizes.at[donor].add(-passed).at[receiver].add(passed)
    labels = jnp.searchsorted(jnp.cumsum(sizes), jnp.arange(rows * top), side="right").astype(jnp.int32)
    grid = labels.reshape(top, rows).T
    grid = grid[jax.random.permutation(jax.random.fold_in(own, 1), rows)]
    rotation = jax.random.randint(jax.random.fold_in(own, 2), (rows, 1), 0, top)
    return jnp.take_along_axis(grid, (jnp.arange(top)[None, :] + rotation) % top, axis=1)


def portions_of(number_of, total, bound, lean, full):
    weights = [(1 << 20) // math.isqrt(rank ** lean) + 1 for rank in range(1, number_of + 1)]
    largest = bound if full else min(bound, max(-(-total // number_of), total * weights[0] // sum(weights)))
    least = 1 if total - largest >= number_of - 1 else 0
    given, surplus = [largest] + [least] * (number_of - 1), total - largest - least * (number_of - 1)
    while surplus > 0:
        movable = [i for i in range(1, number_of) if given[i] < largest] or [i for i in range(1, number_of) if given[i] < bound]
        pool, remaining = sum([weights[i] for i in movable]), surplus
        for i in movable:
            extra = min(bound - given[i], max(1, remaining * weights[i] // pool), surplus)
            given[i] = given[i] + extra
            surplus = surplus - extra
    return np.array(given)


def gaussian(stream_key, dims, width, reach, pieces=(), held_as=jnp.bfloat16):
    drawn = jax.random.normal(stream_key, dims, jnp.float32) * width
    if len(pieces) > 0:
        drawn = block_levels(stream_key, dims, pieces, -0.22, 0.18) * drawn
    return jnp.clip(drawn, min=-reach, max=reach).astype(held_as)


def setup_inputs(seed: int = 0) -> dict:
    keys = jax.random.split(jax.random.key(seed), 7)
    activations = draw_activations(jax.random.fold_in(keys[6], 71), 0)
    routes_keys = jax.random.split(jax.random.fold_in(keys[1], 1), TOKENS // TOK_DEV)
    routes_turns = jax.random.permutation(jax.random.fold_in(keys[1], 3), TOKENS // TOK_DEV)
    routes = jax.vmap(lambda own, number: shared_out(jax.random.fold_in(keys[1], 2), own, number, TOK_DEV, EXPERTS, TOP, CAP, 2))(routes_keys, routes_turns).reshape((TOKENS, TOP))
    owner_map = jax.random.permutation(keys[2], EXPERTS).astype(jnp.int32)
    damp_pct = with_ends(jax.random.randint(keys[3], (EXPERTS,), 5, 21), jax.random.fold_in(keys[3], 1), 5, 20).astype(jnp.int32)
    scale_code = with_ends(jax.random.randint(keys[4], (EXPERTS, D_OUT), 8, 33), jax.random.fold_in(keys[4], 1), 8, 32).astype(jnp.int32)
    weight_panel = gaussian(keys[5], (EXPERTS, PANEL, D_OUT), 1.0, 4.0, ((0, 256),))
    return dict(activations=activations, routes=routes, owner_map=owner_map, damp_pct=damp_pct, scale_code=scale_code, weight_panel=weight_panel)


two_pi = 6.283185307179586

def soft_level(values, step):
    scaled = values / step
    smooth = scaled - jnp.sin(two_pi * scaled) / two_pi
    return step * jnp.clip(smooth, -8.0, 7.0)

def quantize_panel(panel, strip, step):
    size = panel.shape[0]
    head = strip[:, :size]
    positions = jnp.arange(size, dtype=jnp.int32)

    def turn(column, carry):
        current, levels = carry
        values = lax.dynamic_index_in_dim(current, column, 0, keepdims=False)
        head_row = lax.dynamic_index_in_dim(head, column, 0, keepdims=False)
        pivot = lax.dynamic_index_in_dim(head_row, column, 0, keepdims=False)
        level = soft_level(values, step)
        error = (values - level) / pivot
        later = positions > column
        current = current - jnp.where(later, head_row, jnp.zeros_like(head_row))[:, None] * error[None, :]
        levels = lax.dynamic_update_index_in_dim(levels, level, column, 0)
        return (current, levels)
    unused, levels = lax.fori_loop(0, size, turn, (panel, jnp.zeros_like(panel)))
    return levels

def reference(activations, routes, owner_map, damp_pct, scale_code, weight_panel):
    rows_flat = activations.reshape(-1, FF)
    slot_flat = owner_map[routes].reshape(-1).astype(jnp.int32)
    order = jnp.argsort(slot_flat, stable=True).astype(jnp.int32)
    counts = jnp.bincount(slot_flat, length=EXPERTS).astype(jnp.int32)
    starts = (jnp.cumsum(counts) - counts).astype(jnp.int32)
    longest = CAP * N_EXPERT * N_HELP
    padded = jnp.concatenate([order, jnp.zeros((longest,), jnp.int32)])
    factor = 2.0 / (TOK_DEV * TOP)

    def per_slot(slot):
        picks = lax.dynamic_slice(padded, (starts[slot].astype(jnp.int32),), (longest,))
        keep = jnp.arange(longest, dtype=jnp.int32) < counts[slot]
        chosen = jnp.where(keep[:, None], rows_flat[picks], jnp.zeros((), activations.dtype))
        gram = jnp.dot(chosen.T.astype(jnp.float32), chosen.astype(jnp.float32), preferred_element_type=jnp.float32)
        hessian = gram * factor
        strength = damp_pct[slot].astype(jnp.float32) / 100.0
        damped = hessian + strength * jnp.mean(jnp.diagonal(hessian)) * jnp.eye(FF, dtype=jnp.float32)
        lower = jnp.linalg.cholesky(damped)
        leading = jnp.eye(FF, PANEL, dtype=jnp.float32)
        inverse_rows = jax.scipy.linalg.cho_solve((lower, True), leading).T
        head_lower = jnp.linalg.cholesky(inverse_rows[:, :PANEL])
        strip = jax.scipy.linalg.solve_triangular(head_lower, inverse_rows, lower=True)
        step = scale_code[slot].astype(jnp.float32) / 32.0
        levels = quantize_panel(weight_panel[slot].astype(jnp.float32), strip, step)
        return (levels, strip)
    quantized, factor_strip = lax.map(per_slot, jnp.arange(EXPERTS, dtype=jnp.int32))
    return (quantized, factor_strip)
```

```python
import functools

import jax
import jax.numpy as jnp
import numpy as np
from jax import lax
from jax.experimental import pallas as pl
from jax.experimental.pallas import tpu as pltpu
from jax.sharding import PartitionSpec as P

HIGH = lax.Precision.HIGHEST
BLK = 128
GROUP = 32

def _mm(a, b):
    return jnp.dot(a, b, precision=HIGH, preferred_element_type=jnp.float32)


def _lane(v, c):
    return jnp.broadcast_to(v[:, c : c + 1], v.shape[:1] + (BLK,))


def _row(v, s):
    return jnp.broadcast_to(v[s : s + 1, :], (8, v.shape[1]))


def _sweep8(panel, first):
    cols = [_lane(panel, first + j) for j in range(8)]
    a = {(i, j): _row(cols[j], i) for j in range(8) for i in range(j + 1)}
    at = lambda i, j: a[(i, j) if i <= j else (j, i)]
    unit, pivots = {}, {}
    for k in range(7, -1, -1):
        pivots[k] = at(k, k)
        for t in range(k + 1, 8):
            unit[(k, t)] = -at(k, t)
        d = 1.0 / at(k, k)
        b = {i: at(i, k) for i in range(8) if i != k}
        u = {i: b[i] * d for i in b}
        for j in b:
            for i in b:
                if i <= j:
                    a[(i, j)] = a[(i, j)] - u[i] * b[j]
        for i in b:
            a[(i, k) if i <= k else (k, i)] = u[i]
        a[(k, k)] = -d
    sub = lax.broadcasted_iota(jnp.int32, (8, BLK), 0)
    inverse = []
    for s in range(8):
        col = -at(0, s)
        for i in range(1, 8):
            col = jnp.where(sub == i, -at(i, s), col)
        inverse.append(col)
    return inverse, unit, pivots


def negative_inverse(tiles):
    tiles = list(tiles)
    lane = lax.broadcasted_iota(jnp.int32, (8, BLK), 1)
    sub = lax.broadcasted_iota(jnp.int32, (8, BLK), 0)
    for g in range(15, -1, -1):
        first = 8 * g
        inside = (lane >= first) & (lane < first + 8)
        cols, _, _ = _sweep8(tiles[g], first)
        panel = jnp.where(inside, jnp.where(lane - first == sub, -1.0, 0.0), tiles[g])
        solved = sum(cols[s] * _row(panel, s) for s in range(8))
        rows = [_row(solved, s) for s in range(8)]
        for i in range(16):
            if i != g:
                kept = jnp.where(inside, 0.0, tiles[i])
                for s in range(8):
                    kept = kept - _lane(tiles[i], first + s) * rows[s]
                tiles[i] = kept
        tiles[g] = solved
    return tiles


def upper_inverse(tiles):
    tiles = list(tiles)
    lane = lax.broadcasted_iota(jnp.int32, (8, BLK), 1)
    sub = lax.broadcasted_iota(jnp.int32, (8, BLK), 0)
    extra = [jnp.where(lane - 8 * i == sub, 1.0, 0.0) for i in range(16)]
    out = [None] * 16
    for g in range(15, -1, -1):
        first = 8 * g
        cols, unit, pivots = _sweep8(tiles[g], first)
        own = None
        for t in range(8):
            col = jnp.where(sub == t, 1.0, 0.0)
            for s in range(t):
                col = jnp.where(sub == s, unit[(s, t)], col)
            term = col * _row(extra[g], t)
            own = term if own is None else own + term
        scale = lax.rsqrt(pivots[0])
        for s in range(1, 8):
            scale = jnp.where(sub == s, lax.rsqrt(pivots[s]), scale)
        out[g] = own * scale
        solved = sum(cols[s] * _row(tiles[g], s) for s in range(8))
        solved_extra = sum(cols[s] * _row(extra[g], s) for s in range(8))
        rows = [_row(solved, s) for s in range(8)]
        rows_extra = [_row(solved_extra, s) for s in range(8)]
        for i in range(g):
            kept, kept_extra = tiles[i], extra[i]
            for s in range(8):
                c = _lane(tiles[i], first + s)
                kept = kept - c * rows[s]
                kept_extra = kept_extra - c * rows_extra[s]
            tiles[i], extra[i] = kept, kept_extra
    return out


def strip_kernel(damp_ref, gram_ref, strip_ref, coeff_ref, coeff_t_ref, h_ref, inv_ref, *, rows_of):
    width = gram_ref.shape[0]
    blocks = width // BLK
    scale = 2.0 / rows_of
    r = lax.broadcasted_iota(jnp.int32, (BLK, BLK), 0)
    c = lax.broadcasted_iota(jnp.int32, (BLK, BLK), 1)
    diagonal = r == c
    total = jnp.zeros((8, BLK), jnp.float32)
    for k in range(blocks):
        d = jnp.where(diagonal, gram_ref[k * BLK : (k + 1) * BLK, k * BLK : (k + 1) * BLK] * scale, 0.0)
        for i in range(16):
            total = total + d[8 * i : 8 * i + 8]
    strength = damp_ref[0].astype(jnp.float32) / 100.0
    shift = strength * (jnp.sum(total) / width)
    h_ref[...] = gram_ref[...] * scale
    for k in range(blocks):
        at = slice(k * BLK, (k + 1) * BLK)
        h_ref[at, at] = h_ref[at, at] + jnp.where(diagonal, shift, 0.0)

    def eliminate(step, carry):
        k = blocks - 1 - step
        at = pl.multiple_of(k * BLK, BLK)
        mine = pl.ds(at, BLK)
        tiles = negative_inverse([h_ref[pl.ds(at + 8 * i, 8), mine] for i in range(16)])
        for i in range(16):
            inv_ref[8 * i : 8 * i + 8, :] = tiles[i]
        neg = inv_ref[...]
        panel = -_mm(neg, h_ref[mine, :])
        h_ref[mine, :] = panel
        h_ref[mine, mine] = neg
        solved = h_ref[mine, :]

        def above(i, unused):
            rows = pl.ds(pl.multiple_of(i * BLK, BLK), BLK)
            col = h_ref[rows, mine]
            h_ref[rows, mine] = jnp.zeros((BLK, BLK), jnp.float32)
            h_ref[rows, :] = h_ref[rows, :] - _mm(col, h_ref[mine, :])
            return unused

        lax.fori_loop(0, k, above, 0)
        return carry

    lax.fori_loop(0, blocks - 1, eliminate, 0)
    tiles = upper_inverse([h_ref[8 * i : 8 * i + 8, :BLK] for i in range(16)])
    for i in range(16):
        inv_ref[8 * i : 8 * i + 8, :] = tiles[i]
    strip_ref[:, :BLK] = inv_ref[...]
    strip_ref[:, BLK:] = -_mm(inv_ref[...], h_ref[:BLK, BLK:])
    head = inv_ref[...]
    coeff = head / jnp.sum(jnp.where(diagonal, head, 0.0), axis=1, keepdims=True)
    coeff_ref[...] = coeff
    coeff_t_ref[...] = coeff.T


def factor_strip(gram, damp_pct, rows_of):
    width = gram.shape[0]
    return pl.pallas_call(
        functools.partial(strip_kernel, rows_of=rows_of),
        out_shape=[
            jax.ShapeDtypeStruct((BLK, width), jnp.float32),
            jax.ShapeDtypeStruct((BLK, BLK), jnp.float32),
            jax.ShapeDtypeStruct((BLK, BLK), jnp.float32),
        ],
        in_specs=[pl.BlockSpec(memory_space=pltpu.SMEM), pl.BlockSpec(memory_space=pltpu.VMEM)],
        out_specs=[pl.BlockSpec(memory_space=pltpu.VMEM)] * 3,
        scratch_shapes=[pltpu.VMEM((width, width), jnp.float32), pltpu.VMEM((BLK, BLK), jnp.float32)],
        compiler_params=pltpu.CompilerParams(vmem_limit_bytes=40 * 1024 * 1024),
        name="factor_strip",
    )(damp_pct, gram)


def sine_coefficients(degree):
    nodes = np.cos((np.arange(400) + 0.5) * np.pi / 400) * 0.125 + 0.125
    r = np.sqrt(nodes)
    q = np.sin(2 * np.pi * r) / (2 * np.pi) / (r * (1 - 4 * nodes))
    return [float(v) for v in np.polynomial.chebyshev.Chebyshev.fit(nodes, q, degree, domain=[0, 0.25]).convert(kind=np.polynomial.Polynomial).coef]


COEF = sine_coefficients(6)


def _poly(z):
    z2 = z * z
    z4 = z2 * z2
    a = COEF[0] + COEF[1] * z
    b = COEF[2] + COEF[3] * z
    c = COEF[4] + COEF[5] * z
    return (a + b * z2) + (c + COEF[6] * z2) * z4


def level_of(values, step, per_step):
    scaled = values * per_step
    r = scaled - jnp.round(scaled)
    z = r * r
    smooth = scaled - (r * (1.0 - 4.0 * z)) * _poly(z)
    return step * jnp.clip(smooth, -8.0, 7.0)


def quantize_kernel(coeff_ref, coeff_t_ref, panel_ref, code_ref, out_ref, work_ref, lay_ref, err_ref, nat_ref):
    size, width = panel_ref.shape
    tiles = width // BLK
    pad = lay_ref.shape[0] // GROUP
    work_ref[...] = panel_ref[...].astype(jnp.float32)
    step = code_ref[...].astype(jnp.float32) / 32.0
    per_step = 1.0 / step
    for group in range(size // GROUP):
        base = group * GROUP
        for sub in range(GROUP // 8):
            for c in range(tiles):
                lay_ref[pl.ds(sub * 8 * pad + c, 8, stride=pad), :] = work_ref[base + 8 * sub : base + 8 * sub + 8, c * BLK : (c + 1) * BLK]
        for sub in range(GROUP // 8):
            now = [lay_ref[(sub * 8 + r) * pad : (sub * 8 + r) * pad + tiles, :] for r in range(8)]
            for i in range(sub * 8):
                error = err_ref[i * pad : i * pad + tiles, :]
                for r in range(8):
                    now[r] = now[r] - coeff_ref[base + i, base + sub * 8 + r] * error
            for r in range(8):
                row = sub * 8 + r
                level = level_of(now[r], step, per_step)
                error = now[r] - level
                for later in range(r + 1, 8):
                    now[later] = now[later] - coeff_ref[base + row, base + sub * 8 + later] * error
                err_ref[row * pad : row * pad + tiles, :] = error
                lay_ref[row * pad : row * pad + tiles, :] = level
        for sub in range(GROUP // 8):
            for c in range(tiles):
                out_ref[base + 8 * sub : base + 8 * sub + 8, c * BLK : (c + 1) * BLK] = lay_ref[pl.ds(sub * 8 * pad + c, 8, stride=pad), :]
        after = base + GROUP
        if after < size:
            for sub in range(GROUP // 8):
                for c in range(tiles):
                    nat_ref[8 * sub : 8 * sub + 8, c * BLK : (c + 1) * BLK] = err_ref[pl.ds(sub * 8 * pad + c, 8, stride=pad), :]
            lhs = coeff_t_ref[after:, base : base + GROUP]

            def chunk(j, unused):
                at = pl.ds(pl.multiple_of(j * 512, 512), 512)
                work_ref[after:, at] = work_ref[after:, at] - _mm(lhs, nat_ref[:, at])
                return unused

            lax.fori_loop(0, width // 512, chunk, 0)


def quantize(coeff, coeff_t, panel, code):
    size, width = panel.shape
    tiles = width // BLK
    pad = 32
    vm = pl.BlockSpec(memory_space=pltpu.VMEM)
    return pl.pallas_call(
        quantize_kernel,
        out_shape=jax.ShapeDtypeStruct((size, width), jnp.float32),
        in_specs=[pl.BlockSpec(memory_space=pltpu.SMEM), vm, vm, vm],
        out_specs=vm,
        scratch_shapes=[
            pltpu.VMEM((size, width), jnp.float32),
            pltpu.VMEM((GROUP * pad, BLK), jnp.float32),
            pltpu.VMEM((GROUP * pad, BLK), jnp.float32),
            pltpu.VMEM((GROUP, width), jnp.float32),
        ],
        compiler_params=pltpu.CompilerParams(vmem_limit_bytes=40 * 1024 * 1024),
        name="quantize",
    )(coeff, coeff_t, panel, code.reshape(tiles, BLK))


def dispatch(activations, routes, owner_map):
    tok_dev, top_count, hidden_width = activations.shape
    experts = owner_map.shape[0]
    capacity = 2 * tok_dev * top_count // experts
    flat_routes = routes.reshape(-1)
    expert_ids = jnp.arange(experts, dtype=jnp.int32)
    picked = (flat_routes[:, None] == expert_ids[None, :]).astype(jnp.int32)
    slot_ids = jnp.sum(picked * owner_map[None, :], axis=1)
    by_slot = (slot_ids[:, None] == expert_ids[None, :]).astype(jnp.int32)
    running = jnp.cumsum(by_slot, axis=0)
    position = jnp.sum(running * by_slot, axis=1) - 1
    target = slot_ids * capacity + position
    outbound = jnp.zeros((experts * capacity, hidden_width), jnp.bfloat16)
    outbound = outbound.at[target].set(activations.reshape(-1, hidden_width))
    return outbound.reshape(experts, capacity, hidden_width)


def shards(activations, routes, owner_map, damp_pct, scale_code, weight_panel):
    tok_dev, top_count, hidden_width = activations.shape
    outbound = dispatch(activations, routes, owner_map)
    received = lax.all_to_all(outbound, ("expert", "help"), split_axis=0, concat_axis=0, tiled=True)
    rows = received.reshape(-1, hidden_width)
    gram = lax.dot_general(rows, rows, (((0,), (0,)), ((), ())), preferred_element_type=jnp.float32)
    strip, coeff, coeff_t = factor_strip(gram, damp_pct, tok_dev * top_count)
    levels = quantize(coeff, coeff_t, weight_panel[0], scale_code[0])
    return (levels[None], strip[None])


def solution(mesh):
    in_specs = (
        P(("expert", "help"), None, None),
        P(("expert", "help"), None),
        P(),
        P(("expert", "help")),
        P(("expert", "help"), None),
        P(("expert", "help"), None, None),
    )
    out_specs = (P(("expert", "help"), None, None), P(("expert", "help"), None, None))
    return jax.shard_map(shards, mesh=mesh, in_specs=in_specs, out_specs=out_specs, check_vma=False)
```

```python
import functools

import jax
import jax.numpy as jnp
import numpy as np
from jax import lax
from jax.experimental import pallas as pl
from jax.experimental.pallas import tpu as pltpu
from jax.sharding import PartitionSpec as P

BLK = 128
GROUP = 32
PIECES = 1

def _parts(v):
    high = v.astype(jnp.bfloat16)
    rest = v - high.astype(jnp.float32)
    mid = rest.astype(jnp.bfloat16)
    return high, mid, (rest - mid.astype(jnp.float32)).astype(jnp.bfloat16)


def _left(v):
    a, b, c = _parts(v)
    return jnp.concatenate([a, a, b, b, a, c], axis=1)


def _right(v):
    a, b, c = _parts(v)
    return jnp.concatenate([a, b, a, b, c, a], axis=0)


def _dot(a, b):
    return jnp.dot(a, b, preferred_element_type=jnp.float32)


def _total(terms):
    while len(terms) > 1:
        terms = [sum(terms[i : i + 2]) for i in range(0, len(terms), 2)]
    return terms[0]


def _pick(sub, rows):
    pairs = [jnp.where(sub < 2 * i + 1, rows[2 * i], rows[2 * i + 1]) for i in range(4)]
    halves = [jnp.where(sub < 4 * i + 2, pairs[2 * i], pairs[2 * i + 1]) for i in range(2)]
    return jnp.where(sub < 4, halves[0], halves[1])


def _lane(v, c):
    return jnp.broadcast_to(v[:, c : c + 1], v.shape[:1] + (BLK,))


def _row(v, s):
    return jnp.broadcast_to(v[s : s + 1, :], (8, v.shape[1]))


def _sweep8(panel, first, room):
    cols = [_lane(panel, first + j) for j in range(8)]
    for j in range(8):
        room[8 * j : 8 * j + 8, :] = cols[j]
    a = {(i, j): _row(room[8 * j + i : 8 * j + i + 1, :], 0) for j in range(8) for i in range(j + 1)}
    at = lambda i, j: a[(i, j) if i <= j else (j, i)]
    unit, pivots = {}, {}
    for k in range(7, -1, -1):
        pivots[k] = at(k, k)
        for t in range(k + 1, 8):
            unit[(k, t)] = -at(k, t)
        d = 1.0 / at(k, k)
        b = {i: at(i, k) for i in range(8) if i != k}
        u = {i: b[i] * d for i in b}
        for j in b:
            for i in b:
                if i <= j:
                    a[(i, j)] = a[(i, j)] - u[i] * b[j]
        for i in b:
            a[(i, k) if i <= k else (k, i)] = u[i]
        a[(k, k)] = -d
    sub = lax.broadcasted_iota(jnp.int32, (8, BLK), 0)
    inverse = []
    for s in range(8):
        inverse.append(-_pick(sub, [at(i, s) for i in range(8)]))
    return inverse, unit, pivots


def negative_inverse(tiles, rooms, beside):
    tiles = list(tiles)
    lane = lax.broadcasted_iota(jnp.int32, (8, BLK), 1)
    sub = lax.broadcasted_iota(jnp.int32, (8, BLK), 0)
    for g in range(15, -1, -1):
        first = 8 * g
        inside = (lane >= first) & (lane < first + 8)
        cols, _, _ = _sweep8(tiles[g], first, rooms.at[g])
        panel = jnp.where(inside, jnp.where(lane - first == sub, -1.0, 0.0), tiles[g])
        room = rooms.at[g]
        room[64:72, :] = panel
        solved = _total([cols[s] * _row(room[64 + s : 65 + s, :], 0) for s in range(8)])
        room[72:80, :] = solved
        rows = [_row(room[72 + s : 73 + s, :], 0) for s in range(8)]
        for i in [g - 1] * (g > 0) + [i for i in range(16) if i != g and i != g - 1]:
            if i != g:
                kept = jnp.where(inside, 0.0, tiles[i])
                terms = [_lane(tiles[i], first + s) * rows[s] for s in range(8)]
                if i == g - 1:
                    kept = kept - _total(terms)
                else:
                    for term in terms:
                        kept = kept - term
                tiles[i] = kept
        tiles[g] = solved
        beside(15 - g)
    return tiles


def upper_inverse(tiles, rooms, beside):
    tiles = list(tiles)
    lane = lax.broadcasted_iota(jnp.int32, (8, BLK), 1)
    sub = lax.broadcasted_iota(jnp.int32, (8, BLK), 0)
    extra = [jnp.where(lane - 8 * i == sub, 1.0, 0.0) for i in range(16)]
    out = [None] * 16
    for g in range(15, -1, -1):
        first = 8 * g
        cols, unit, pivots = _sweep8(tiles[g], first, rooms.at[g])
        own = None
        room = rooms.at[g]
        room[64:72, :] = extra[g]
        for t in range(8):
            col = jnp.where(sub == t, 1.0, 0.0)
            for s in range(t):
                col = jnp.where(sub == s, unit[(s, t)], col)
            term = col * _row(room[64 + t : 65 + t, :], 0)
            own = term if own is None else own + term
        scale = lax.rsqrt(pivots[0])
        for s in range(1, 8):
            scale = jnp.where(sub == s, lax.rsqrt(pivots[s]), scale)
        out[g] = own * scale
        room[72:80, :] = tiles[g]
        solved = _total([cols[s] * _row(room[72 + s : 73 + s, :], 0) for s in range(8)])
        solved_extra = _total([cols[s] * _row(room[64 + s : 65 + s, :], 0) for s in range(8)])
        room[80:88, :] = solved
        room[88:96, :] = solved_extra
        rows = [_row(room[80 + s : 81 + s, :], 0) for s in range(8)]
        rows_extra = [_row(room[88 + s : 89 + s, :], 0) for s in range(8)]
        for i in range(g - 1, -1, -1):
            lanes = [_lane(tiles[i], first + s) for s in range(8)]
            tiles[i] = tiles[i] - _total([lanes[s] * rows[s] for s in range(8)])
            extra[i] = extra[i] - _total([lanes[s] * rows_extra[s] for s in range(8)])
        beside(15 - g)
    return out


def strip_kernel(damp_ref, *refs, rows_of, pieces):
    gram_refs, refs = refs[:pieces], refs[pieces:]
    strip_ref, coeff_ref, coeff_t_ref, h_ref, inv_ref, rooms, block_ref, neg_ref, left_ref, right_ref = refs
    width = gram_refs[0].shape[0]
    blocks = width // BLK
    scale = 2.0 / rows_of
    r = lax.broadcasted_iota(jnp.int32, (BLK, BLK), 0)
    c = lax.broadcasted_iota(jnp.int32, (BLK, BLK), 1)
    diagonal = r == c
    h_ref[...] = sum(ref[...] for ref in gram_refs) * scale
    total = jnp.zeros((8, BLK), jnp.float32)
    for k in range(blocks):
        d = jnp.where(diagonal, h_ref[k * BLK : (k + 1) * BLK, k * BLK : (k + 1) * BLK], 0.0)
        for i in range(16):
            total = total + d[8 * i : 8 * i + 8]
    strength = damp_ref[0].astype(jnp.float32) / 100.0
    shift = strength * (jnp.sum(total) / width)
    for k in range(blocks):
        at = slice(k * BLK, (k + 1) * BLK)
        h_ref[at, at] = h_ref[at, at] + jnp.where(diagonal, shift, 0.0)

    def keep(tiles):
        for i in range(16):
            inv_ref[8 * i : 8 * i + 8, :] = tiles[i]

    def turn(k, reach, invert):
        last = k + 1
        mine, theirs = [pl.ds(pl.multiple_of(b * BLK, BLK), BLK) for b in (k, last)]
        neg = inv_ref[...]
        neg_left = _left(neg)
        lead = -_dot(neg_left, _right(h_ref[theirs, mine]))
        block_ref[...] = h_ref[mine, mine] - _dot(_left(h_ref[mine, theirs]), _right(lead))
        neg_ref[...] = neg_left
        for i in range(reach):
            rows = slice(i * BLK, (i + 1) * BLK)
            col = h_ref[rows, theirs]
            left_ref[rows, :] = _left(jnp.where(i < last, col, 0.0))
            h_ref[rows, theirs] = jnp.where(i < last, 0.0, col)
        chunk = width // 4
        part = reach * BLK // 4

        def beside(piece):
            at = slice(piece // 4 * chunk, (piece // 4 + 1) * chunk)
            if piece % 4 == 0:
                solved = -_dot(neg_ref[...], _right(h_ref[theirs, at]))
                place = lax.broadcasted_iota(jnp.int32, (BLK, chunk), 1) + at.start
                own = (place >= last * BLK) & (place < last * BLK + BLK)
                solved = jnp.where(own, jnp.concatenate([neg] * (chunk // BLK), axis=1), solved)
                right_ref[:, at] = _right(solved)
            rows = slice(piece % 4 * part, (piece % 4 + 1) * part)
            h_ref[rows, at] = h_ref[rows, at] - _dot(left_ref[rows, :], right_ref[:, at])

        return invert([block_ref[8 * i : 8 * i + 8, :] for i in range(16)], rooms, beside)

    def sweep_block(reach, first):
        def step(s, carry):
            keep(turn(first - s, reach, negative_inverse))
            return carry

        return step

    corner = (blocks - 1) * BLK
    keep(negative_inverse([h_ref[corner + 8 * i : corner + 8 * i + 8, corner:] for i in range(16)], rooms, lambda piece: None))
    half = blocks // 2
    lax.fori_loop(0, half - 1, sweep_block(blocks - 1, blocks - 2), 0)
    lax.fori_loop(0, half - 1, sweep_block(half, half - 1), 0)
    keep(turn(0, 1, upper_inverse))
    strip_ref[:, :BLK] = inv_ref[...]
    strip_ref[:, BLK:] = -_dot(_left(inv_ref[...]), _right(h_ref[:BLK, BLK:]))
    head = inv_ref[...]
    coeff = head / jnp.sum(jnp.where(diagonal, head, 0.0), axis=1, keepdims=True)
    coeff_ref[...] = coeff
    coeff_t_ref[...] = coeff.T


def factor_strip(grams, damp_pct, rows_of):
    width = grams[0].shape[0]
    return pl.pallas_call(
        functools.partial(strip_kernel, rows_of=rows_of, pieces=len(grams)),
        out_shape=[
            jax.ShapeDtypeStruct((BLK, width), jnp.float32),
            jax.ShapeDtypeStruct((BLK, BLK), jnp.float32),
            jax.ShapeDtypeStruct((BLK, BLK), jnp.float32),
        ],
        in_specs=[pl.BlockSpec(memory_space=pltpu.SMEM)] + [pl.BlockSpec(memory_space=pltpu.VMEM)] * len(grams),
        out_specs=[pl.BlockSpec(memory_space=pltpu.VMEM)] * 3,
        scratch_shapes=[pltpu.VMEM((width, width), jnp.float32), pltpu.VMEM((BLK, BLK), jnp.float32), pltpu.VMEM((16, 96, BLK), jnp.float32), pltpu.VMEM((BLK, BLK), jnp.float32), pltpu.VMEM((BLK, 6 * BLK), jnp.bfloat16), pltpu.VMEM((width - BLK, 6 * BLK), jnp.bfloat16), pltpu.VMEM((6 * BLK, width), jnp.bfloat16)],
        compiler_params=pltpu.CompilerParams(vmem_limit_bytes=40 * 1024 * 1024),
        name="factor_strip",
    )(damp_pct, *grams)


def sine_coefficients(degree):
    nodes = np.cos((np.arange(400) + 0.5) * np.pi / 400) * 0.125 + 0.125
    r = np.sqrt(nodes)
    q = np.sin(2 * np.pi * r) / (2 * np.pi) / (r * (1 - 4 * nodes))
    return [float(v) for v in np.polynomial.chebyshev.Chebyshev.fit(nodes, q, degree, domain=[0, 0.25]).convert(kind=np.polynomial.Polynomial).coef]


COEF = sine_coefficients(5)


def _poly(z):
    z2 = z * z
    z4 = z2 * z2
    a = COEF[0] + COEF[1] * z
    b = COEF[2] + COEF[3] * z
    c = COEF[4] + COEF[5] * z
    return (a + b * z2) + c * z4


def level_of(values, step, per_step):
    scaled = values * per_step
    r = scaled - jnp.round(scaled)
    z = r * r
    smooth = scaled - (r * (1.0 - 4.0 * z)) * _poly(z)
    return step * jnp.clip(smooth, -8.0, 7.0)


def quantize_kernel(coeff_ref, coeff_t_ref, panel_ref, code_ref, out_ref, work_ref, lay_ref, err_ref, nat_ref, left_ref):
    size, width = panel_ref.shape
    tiles = width // BLK
    pad = lay_ref.shape[0] // GROUP
    work_ref[...] = panel_ref[...].astype(jnp.float32)
    step = code_ref[...].astype(jnp.float32) / 32.0
    per_step = 1.0 / step
    for group in range(size // GROUP):
        base = group * GROUP
        for sub in range(GROUP // 8):
            for c in range(tiles):
                lay_ref[pl.ds(sub * 8 * pad + c, 8, stride=pad), :] = work_ref[base + 8 * sub : base + 8 * sub + 8, c * BLK : (c + 1) * BLK]
        for sub in range(GROUP // 8):
            now = [lay_ref[(sub * 8 + r) * pad : (sub * 8 + r) * pad + tiles, :] for r in range(8)]
            for i in range(sub * 8):
                error = err_ref[i * pad : i * pad + tiles, :]
                for r in range(8):
                    now[r] = now[r] - coeff_ref[base + i, base + sub * 8 + r] * error
            for r in range(8):
                row = sub * 8 + r
                level = level_of(now[r], step, per_step)
                error = now[r] - level
                for later in range(r + 1, 8):
                    now[later] = now[later] - coeff_ref[base + row, base + sub * 8 + later] * error
                err_ref[row * pad : row * pad + tiles, :] = error
                lay_ref[row * pad : row * pad + tiles, :] = level
        for sub in range(GROUP // 8):
            for c in range(tiles):
                out_ref[base + 8 * sub : base + 8 * sub + 8, c * BLK : (c + 1) * BLK] = lay_ref[pl.ds(sub * 8 * pad + c, 8, stride=pad), :]
        after = base + GROUP
        if after < size:
            for sub in range(GROUP // 8):
                for c in range(tiles):
                    nat_ref[8 * sub : 8 * sub + 8, c * BLK : (c + 1) * BLK] = err_ref[pl.ds(sub * 8 * pad + c, 8, stride=pad), :]
            left_ref[after:, :] = _left(coeff_t_ref[after:, base : base + GROUP])

            def chunk(j, unused):
                at = pl.ds(pl.multiple_of(j * 512, 512), 512)
                work_ref[after:, at] = work_ref[after:, at] - _dot(left_ref[after:, :], _right(nat_ref[:, at]))
                return unused

            lax.fori_loop(0, width // 512, chunk, 0)


def quantize(coeff, coeff_t, panel, code):
    size, width = panel.shape
    tiles = width // BLK
    pad = 32
    vm = pl.BlockSpec(memory_space=pltpu.VMEM)
    return pl.pallas_call(
        quantize_kernel,
        out_shape=jax.ShapeDtypeStruct((size, width), jnp.float32),
        in_specs=[pl.BlockSpec(memory_space=pltpu.SMEM), vm, vm, vm],
        out_specs=vm,
        scratch_shapes=[
            pltpu.VMEM((size, width), jnp.float32),
            pltpu.VMEM((GROUP * pad, BLK), jnp.float32),
            pltpu.VMEM((GROUP * pad, BLK), jnp.float32),
            pltpu.VMEM((GROUP, width), jnp.float32),
            pltpu.VMEM((size, 6 * GROUP), jnp.bfloat16),
        ],
        compiler_params=pltpu.CompilerParams(vmem_limit_bytes=40 * 1024 * 1024),
        name="quantize",
    )(coeff, coeff_t, panel, code.reshape(tiles, BLK))


def destinations(routes, owner_map):
    experts = owner_map.shape[0]
    flat_routes = routes.reshape(-1)
    expert_ids = jnp.arange(experts, dtype=jnp.int32)
    picked = (flat_routes[:, None] == expert_ids[None, :]).astype(jnp.int32)
    slot_ids = jnp.sum(picked * owner_map[None, :], axis=1)
    by_slot = (slot_ids[:, None] == expert_ids[None, :]).astype(jnp.int32)
    running = jnp.cumsum(by_slot, axis=0)
    return slot_ids, jnp.sum(running * by_slot, axis=1) - 1


def shards(activations, routes, owner_map, damp_pct, scale_code, weight_panel):
    tok_dev, top_count, hidden_width = activations.shape
    experts = owner_map.shape[0]
    capacity = 2 * tok_dev * top_count // experts // PIECES
    slot_ids, position = destinations(routes, owner_map)
    sent = activations.reshape(-1, hidden_width)
    grams = []
    for piece in range(PIECES):
        place = position - piece * capacity
        target = jnp.where((place >= 0) & (place < capacity), slot_ids * capacity + place, experts * capacity)
        outbound = jnp.zeros((experts * capacity, hidden_width), jnp.bfloat16)
        outbound = outbound.at[target].set(sent, mode="drop", unique_indices=False)
        outbound = outbound.reshape(experts, capacity, hidden_width)
        received = lax.all_to_all(outbound, ("expert", "help"), split_axis=0, concat_axis=0, tiled=True)
        rows = received.reshape(-1, hidden_width)
        grams.append(lax.dot_general(rows, rows, (((0,), (0,)), ((), ())), preferred_element_type=jnp.float32))
    strip, coeff, coeff_t = factor_strip(grams, damp_pct, tok_dev * top_count)
    levels = quantize(coeff, coeff_t, weight_panel[0], scale_code[0])
    return (levels[None], strip[None])


def solution(mesh):
    in_specs = (
        P(("expert", "help"), None, None),
        P(("expert", "help"), None),
        P(),
        P(("expert", "help")),
        P(("expert", "help"), None),
        P(("expert", "help"), None, None),
    )
    out_specs = (P(("expert", "help"), None, None), P(("expert", "help"), None, None))
    return jax.shard_map(shards, mesh=mesh, in_specs=in_specs, out_specs=out_specs, check_vma=False)
```

```python
import functools

import jax
import jax.numpy as jnp
import numpy as np
from jax import lax
from jax.experimental import pallas as pl
from jax.experimental.pallas import tpu as pltpu
from jax.sharding import PartitionSpec as P

BLK = 128
GROUP = 32

def _parts(v):
    high = v.astype(jnp.bfloat16)
    rest = v - high.astype(jnp.float32)
    mid = rest.astype(jnp.bfloat16)
    return high, mid, (rest - mid.astype(jnp.float32)).astype(jnp.bfloat16)


def _left(v):
    a, b, c = _parts(v)
    return jnp.concatenate([a, a, b, b, a, c], axis=1)


def _right(v):
    a, b, c = _parts(v)
    return jnp.concatenate([a, b, a, b, c, a], axis=0)


def _dot(a, b):
    return jnp.dot(a, b, preferred_element_type=jnp.float32)


def _total(terms):
    while len(terms) > 1:
        terms = [sum(terms[i : i + 2]) for i in range(0, len(terms), 2)]
    return terms[0]


def _pick(sub, rows):
    pairs = [jnp.where(sub < 2 * i + 1, rows[2 * i], rows[2 * i + 1]) for i in range(4)]
    halves = [jnp.where(sub < 4 * i + 2, pairs[2 * i], pairs[2 * i + 1]) for i in range(2)]
    return jnp.where(sub < 4, halves[0], halves[1])


def _lane(v, c):
    return jnp.broadcast_to(v[:, c : c + 1], v.shape[:1] + (BLK,))


def _row(v, s):
    return jnp.broadcast_to(v[s : s + 1, :], (8, v.shape[1]))


def _sweep8(panel, first, room):
    cols = [_lane(panel, first + j) for j in range(8)]
    for j in range(8):
        room[8 * j : 8 * j + 8, :] = cols[j]
    a = {(i, j): _row(room[8 * j + i : 8 * j + i + 1, :], 0) for j in range(8) for i in range(j + 1)}
    at = lambda i, j: a[(i, j) if i <= j else (j, i)]
    unit, pivots = {}, {}
    for k in range(7, -1, -1):
        pivots[k] = at(k, k)
        for t in range(k + 1, 8):
            unit[(k, t)] = -at(k, t)
        d = 1.0 / at(k, k)
        b = {i: at(i, k) for i in range(8) if i != k}
        u = {i: b[i] * d for i in b}
        for j in b:
            for i in b:
                if i <= j:
                    a[(i, j)] = a[(i, j)] - u[i] * b[j]
        for i in b:
            a[(i, k) if i <= k else (k, i)] = u[i]
        a[(k, k)] = -d
    sub = lax.broadcasted_iota(jnp.int32, (8, BLK), 0)
    inverse = []
    for s in range(8):
        inverse.append(-_pick(sub, [at(i, s) for i in range(8)]))
    return inverse, unit, pivots


def negative_inverse(tiles, rooms, beside):
    tiles = list(tiles)
    lane = lax.broadcasted_iota(jnp.int32, (8, BLK), 1)
    sub = lax.broadcasted_iota(jnp.int32, (8, BLK), 0)
    for g in range(15, -1, -1):
        first = 8 * g
        inside = (lane >= first) & (lane < first + 8)
        cols, _, _ = _sweep8(tiles[g], first, rooms.at[g])
        panel = jnp.where(inside, jnp.where(lane - first == sub, -1.0, 0.0), tiles[g])
        room = rooms.at[g]
        room[64:72, :] = panel
        solved = _total([cols[s] * _row(room[64 + s : 65 + s, :], 0) for s in range(8)])
        room[72:80, :] = solved
        rows = [_row(room[72 + s : 73 + s, :], 0) for s in range(8)]
        for i in [g - 1] * (g > 0) + [i for i in range(16) if i != g and i != g - 1]:
            if i != g:
                kept = jnp.where(inside, 0.0, tiles[i])
                terms = [_lane(tiles[i], first + s) * rows[s] for s in range(8)]
                if i == g - 1:
                    kept = kept - _total(terms)
                else:
                    for term in terms:
                        kept = kept - term
                tiles[i] = kept
        tiles[g] = solved
        beside(15 - g)
    return tiles


def upper_inverse(tiles, rooms, beside):
    tiles = list(tiles)
    lane = lax.broadcasted_iota(jnp.int32, (8, BLK), 1)
    sub = lax.broadcasted_iota(jnp.int32, (8, BLK), 0)
    extra = [jnp.where(lane - 8 * i == sub, 1.0, 0.0) for i in range(16)]
    out = [None] * 16
    for g in range(15, -1, -1):
        first = 8 * g
        cols, unit, pivots = _sweep8(tiles[g], first, rooms.at[g])
        own = None
        room = rooms.at[g]
        room[64:72, :] = extra[g]
        for t in range(8):
            col = jnp.where(sub == t, 1.0, 0.0)
            for s in range(t):
                col = jnp.where(sub == s, unit[(s, t)], col)
            term = col * _row(room[64 + t : 65 + t, :], 0)
            own = term if own is None else own + term
        scale = lax.rsqrt(pivots[0])
        for s in range(1, 8):
            scale = jnp.where(sub == s, lax.rsqrt(pivots[s]), scale)
        out[g] = own * scale
        room[72:80, :] = tiles[g]
        solved = _total([cols[s] * _row(room[72 + s : 73 + s, :], 0) for s in range(8)])
        solved_extra = _total([cols[s] * _row(room[64 + s : 65 + s, :], 0) for s in range(8)])
        room[80:88, :] = solved
        room[88:96, :] = solved_extra
        rows = [_row(room[80 + s : 81 + s, :], 0) for s in range(8)]
        rows_extra = [_row(room[88 + s : 89 + s, :], 0) for s in range(8)]
        for i in range(g - 1, -1, -1):
            lanes = [_lane(tiles[i], first + s) for s in range(8)]
            tiles[i] = tiles[i] - _total([lanes[s] * rows[s] for s in range(8)])
            extra[i] = extra[i] - _total([lanes[s] * rows_extra[s] for s in range(8)])
        beside(15 - g)
    return out


def strip_kernel(damp_ref, rows_ref, strip_ref, coeff_ref, coeff_t_ref, h_ref, *scratch, rows_of):
    step = pl.program_id(0)

    @pl.when(step == 0)
    def clear():
        h_ref[...] = jnp.zeros_like(h_ref)

    width = rows_ref.shape[1]
    quarter = width // 4
    for first in range(0, width, quarter):
        own = rows_ref[:, first : first + quarter]
        h_ref[first : first + quarter, first:] += lax.dot_general(
            own, rows_ref[:, first:], (((0,), (0,)), ((), ())), preferred_element_type=jnp.float32
        )

    @pl.when(step == pl.num_programs(0) - 1)
    def finish():
        eliminate(damp_ref, strip_ref, coeff_ref, coeff_t_ref, h_ref, *scratch, rows_of)


def eliminate(damp_ref, strip_ref, coeff_ref, coeff_t_ref, h_ref, inv_ref, rooms, block_ref, neg_ref, left_ref, right_ref, rows_of):
    width = h_ref.shape[0]
    blocks = width // BLK
    quarter = width // 4
    scale = 2.0 / rows_of
    r = lax.broadcasted_iota(jnp.int32, (BLK, BLK), 0)
    c = lax.broadcasted_iota(jnp.int32, (BLK, BLK), 1)
    diagonal = r == c
    for first in range(0, width, quarter):
        above = slice(first, first + quarter)
        h_ref[above, first:] = h_ref[above, first:] * scale
        for later in range(first + quarter, width, quarter):
            h_ref[later : later + quarter, above] = h_ref[above, later : later + quarter].T
    total = jnp.zeros((8, BLK), jnp.float32)
    for k in range(blocks):
        d = jnp.where(diagonal, h_ref[k * BLK : (k + 1) * BLK, k * BLK : (k + 1) * BLK], 0.0)
        for i in range(16):
            total = total + d[8 * i : 8 * i + 8]
    strength = damp_ref[0].astype(jnp.float32) / 100.0
    shift = strength * (jnp.sum(total) / width)
    for k in range(blocks):
        at = slice(k * BLK, (k + 1) * BLK)
        h_ref[at, at] = h_ref[at, at] + jnp.where(diagonal, shift, 0.0)

    def keep(tiles):
        for i in range(16):
            inv_ref[8 * i : 8 * i + 8, :] = tiles[i]

    def turn(k, reach, invert):
        last = k + 1
        mine, theirs = [pl.ds(pl.multiple_of(b * BLK, BLK), BLK) for b in (k, last)]
        neg = inv_ref[...]
        neg_left = _left(neg)
        lead = -_dot(neg_left, _right(h_ref[theirs, mine]))
        block_ref[...] = h_ref[mine, mine] - _dot(_left(h_ref[mine, theirs]), _right(lead))
        neg_ref[...] = neg_left
        for i in range(reach):
            rows = slice(i * BLK, (i + 1) * BLK)
            col = h_ref[rows, theirs]
            left_ref[rows, :] = _left(jnp.where(i < last, col, 0.0))
            h_ref[rows, theirs] = jnp.where(i < last, 0.0, col)
        chunk = width // 4
        part = reach * BLK // 4

        def beside(piece):
            at = slice(piece // 4 * chunk, (piece // 4 + 1) * chunk)
            if piece % 4 == 0:
                solved = -_dot(neg_ref[...], _right(h_ref[theirs, at]))
                place = lax.broadcasted_iota(jnp.int32, (BLK, chunk), 1) + at.start
                own = (place >= last * BLK) & (place < last * BLK + BLK)
                solved = jnp.where(own, jnp.concatenate([neg] * (chunk // BLK), axis=1), solved)
                right_ref[:, at] = _right(solved)
            rows = slice(piece % 4 * part, (piece % 4 + 1) * part)
            h_ref[rows, at] = h_ref[rows, at] - _dot(left_ref[rows, :], right_ref[:, at])

        return invert([block_ref[8 * i : 8 * i + 8, :] for i in range(16)], rooms, beside)

    def sweep_block(reach, first):
        def step(s, carry):
            keep(turn(first - s, reach, negative_inverse))
            return carry

        return step

    corner = (blocks - 1) * BLK
    keep(negative_inverse([h_ref[corner + 8 * i : corner + 8 * i + 8, corner:] for i in range(16)], rooms, lambda piece: None))
    half = blocks // 2
    lax.fori_loop(0, half - 1, sweep_block(blocks - 1, blocks - 2), 0)
    lax.fori_loop(0, half - 1, sweep_block(half, half - 1), 0)
    keep(turn(0, 1, upper_inverse))
    strip_ref[:, :BLK] = inv_ref[...]
    strip_ref[:, BLK:] = -_dot(_left(inv_ref[...]), _right(h_ref[:BLK, BLK:]))
    head = inv_ref[...]
    coeff = head / jnp.sum(jnp.where(diagonal, head, 0.0), axis=1, keepdims=True)
    coeff_ref[...] = coeff
    coeff_t_ref[...] = coeff.T


def factor_strip(rows, damp_pct, rows_of):
    count, width = rows.shape
    block = 1024
    whole = lambda shape: pl.BlockSpec(shape, lambda i: (0, 0))
    f32, bf16 = jnp.float32, jnp.bfloat16
    return pl.pallas_call(
        functools.partial(strip_kernel, rows_of=rows_of),
        grid=(count // block,),
        out_shape=[jax.ShapeDtypeStruct(shape, f32) for shape in ((BLK, width), (BLK, BLK), (BLK, BLK))],
        in_specs=[pl.BlockSpec(memory_space=pltpu.SMEM), pl.BlockSpec((block, width), lambda i: (i, 0))],
        out_specs=[whole((BLK, width)), whole((BLK, BLK)), whole((BLK, BLK))],
        scratch_shapes=[
            pltpu.VMEM((width, width), f32),
            pltpu.VMEM((BLK, BLK), f32),
            pltpu.VMEM((16, 96, BLK), f32),
            pltpu.VMEM((BLK, BLK), f32),
            pltpu.VMEM((BLK, 6 * BLK), bf16),
            pltpu.VMEM((width - BLK, 6 * BLK), bf16),
            pltpu.VMEM((6 * BLK, width), bf16),
        ],
        compiler_params=pltpu.CompilerParams(vmem_limit_bytes=40 * 1024 * 1024),
        name="factor_strip",
    )(damp_pct, rows)


def sine_coefficients(degree):
    nodes = np.cos((np.arange(400) + 0.5) * np.pi / 400) * 0.125 + 0.125
    r = np.sqrt(nodes)
    q = np.sin(2 * np.pi * r) / (2 * np.pi) / (r * (1 - 4 * nodes))
    return [float(v) for v in np.polynomial.chebyshev.Chebyshev.fit(nodes, q, degree, domain=[0, 0.25]).convert(kind=np.polynomial.Polynomial).coef]


COEF = sine_coefficients(5)


def _poly(z):
    z2 = z * z
    z4 = z2 * z2
    a = COEF[0] + COEF[1] * z
    b = COEF[2] + COEF[3] * z
    c = COEF[4] + COEF[5] * z
    return (a + b * z2) + c * z4


def level_of(values, step, per_step):
    scaled = values * per_step
    r = scaled - jnp.round(scaled)
    z = r * r
    smooth = scaled - (r * (1.0 - 4.0 * z)) * _poly(z)
    return step * jnp.clip(smooth, -8.0, 7.0)


def quantize_kernel(coeff_ref, coeff_t_ref, panel_ref, code_ref, out_ref, work_ref, lay_ref, err_ref, nat_ref, left_ref):
    size, width = panel_ref.shape
    tiles = width // BLK
    pad = lay_ref.shape[0] // (GROUP + 1)
    work_ref[...] = panel_ref[...].astype(jnp.float32)
    step = code_ref[...].astype(jnp.float32) / 32.0
    per_step = 1.0 / step
    for group in range(size // GROUP):
        base = group * GROUP
        for sub in range(GROUP // 8):
            for c in range(tiles):
                lay_ref[pl.ds(sub * 8 * pad + c, 8, stride=pad), :] = work_ref[base + 8 * sub : base + 8 * sub + 8, c * BLK : (c + 1) * BLK]
        for sub in range(GROUP // 8):
            now = [lay_ref[(sub * 8 + r) * pad : (sub * 8 + r) * pad + tiles, :] for r in range(8)]
            for i in range(sub * 8):
                error = err_ref[i * pad : i * pad + tiles, :]
                for r in range(8):
                    now[r] = now[r] - coeff_ref[base + i, base + sub * 8 + r] * error
            for r in range(8):
                row = sub * 8 + r
                level = level_of(now[r], step, per_step)
                error = now[r] - level
                for later in range(r + 1, 8):
                    now[later] = now[later] - coeff_ref[base + row, base + sub * 8 + later] * error
                err_ref[row * pad : row * pad + tiles, :] = error
                lay_ref[row * pad : row * pad + tiles, :] = level
        for sub in range(GROUP // 8):
            for c in range(tiles):
                out_ref[base + 8 * sub : base + 8 * sub + 8, c * BLK : (c + 1) * BLK] = lay_ref[pl.ds(sub * 8 * pad + c, 8, stride=pad), :]
        after = base + GROUP
        if after < size:
            for sub in range(GROUP // 8):
                for c in range(tiles):
                    nat_ref[8 * sub : 8 * sub + 8, c * BLK : (c + 1) * BLK] = err_ref[pl.ds(sub * 8 * pad + c, 8, stride=pad), :]
            left_ref[after:, :] = _left(coeff_t_ref[after:, base : base + GROUP])

            def chunk(j, unused):
                at = pl.ds(pl.multiple_of(j * 512, 512), 512)
                work_ref[after:, at] = work_ref[after:, at] - _dot(left_ref[after:, :], _right(nat_ref[:, at]))
                return unused

            lax.fori_loop(0, width // 512, chunk, 0)


def quantize(coeff, coeff_t, panel, code):
    size, width = panel.shape
    tiles = width // BLK
    pad = 32
    vm = pl.BlockSpec(memory_space=pltpu.VMEM)
    return pl.pallas_call(
        quantize_kernel,
        out_shape=jax.ShapeDtypeStruct((size, width), jnp.float32),
        in_specs=[pl.BlockSpec(memory_space=pltpu.SMEM), vm, vm, vm],
        out_specs=vm,
        scratch_shapes=[
            pltpu.VMEM((size, width), jnp.float32),
            pltpu.VMEM((GROUP * pad + pad, BLK), jnp.float32),
            pltpu.VMEM((GROUP * pad + pad, BLK), jnp.float32),
            pltpu.VMEM((GROUP, width), jnp.float32),
            pltpu.VMEM((size, 6 * GROUP), jnp.bfloat16),
        ],
        compiler_params=pltpu.CompilerParams(vmem_limit_bytes=40 * 1024 * 1024),
        name="quantize",
    )(coeff, coeff_t, panel, code.reshape(tiles, BLK))


def destinations(routes, owner_map):
    experts = owner_map.shape[0]
    flat_routes = routes.reshape(-1)
    expert_ids = jnp.arange(experts, dtype=jnp.int32)
    picked = (flat_routes[:, None] == expert_ids[None, :]).astype(jnp.int32)
    slot_ids = jnp.sum(picked * owner_map[None, :], axis=1)
    by_slot = (slot_ids[:, None] == expert_ids[None, :]).astype(jnp.int32)
    running = jnp.cumsum(by_slot, axis=0)
    return slot_ids, jnp.sum(running * by_slot, axis=1) - 1


def bucket_kernel(target_ref, sent_ref, out_ref, line_ref, slots_ref, *, half):
    step = pl.program_id(0)
    across = sent_ref.shape[1] // BLK

    @pl.when(step == 0)
    def clear():
        def some(i, unused):
            slots_ref[pl.ds(pl.multiple_of(i * 512, 512), 512), :] = jnp.zeros((512, BLK), jnp.float32)
            return unused

        lax.fori_loop(0, slots_ref.shape[0] // 512, some, 0)

    @pl.when(step < half)
    def put():
        def some(i, unused):
            for part in range(4):
                first = pl.multiple_of(i * 64 + part * 16, 16)
                line = line_ref.at[part]
                for c in range(across):
                    line[pl.ds(c, 16, stride=across), :] = sent_ref[pl.ds(first, 16), c * BLK : (c + 1) * BLK].astype(jnp.float32)
                for r in range(16):
                    place = target_ref[step * sent_ref.shape[0] + first + r]
                    slots_ref[pl.ds(pl.multiple_of(place * across, across), across), :] = line[r * across : (r + 1) * across, :]
            return unused

        lax.fori_loop(0, sent_ref.shape[0] // 64, some, 0)

    @pl.when(step >= half)
    def take():
        begin = (step - half) * out_ref.shape[0]

        def some(i, unused):
            for part in range(4):
                first = pl.multiple_of(i * 64 + part * 16, 16)
                for c in range(across):
                    rows = slots_ref[pl.ds((begin + first) * across + c, 16, stride=across), :]
                    out_ref[pl.ds(first, 16), c * BLK : (c + 1) * BLK] = rows.astype(jnp.bfloat16)
            return unused

        lax.fori_loop(0, out_ref.shape[0] // 64, some, 0)


def bucket(sent, target, places):
    count, width = sent.shape
    steps, writes = 2, 4
    across = width // BLK
    return pl.pallas_call(
        functools.partial(bucket_kernel, half=steps),
        grid=(steps + writes,),
        out_shape=jax.ShapeDtypeStruct((places, width), jnp.bfloat16),
        in_specs=[
            pl.BlockSpec(memory_space=pltpu.SMEM),
            pl.BlockSpec((count // steps, width), lambda i: (jnp.minimum(i, steps - 1), 0)),
        ],
        out_specs=pl.BlockSpec((places // writes, width), lambda i: (jnp.maximum(i - steps, 0), 0)),
        scratch_shapes=[pltpu.VMEM((4, 17 * across, BLK), jnp.float32), pltpu.VMEM((places * across + across, BLK), jnp.float32)],
        compiler_params=pltpu.CompilerParams(vmem_limit_bytes=40 * 1024 * 1024),
        name="bucket",
    )(target, sent)


def shards(activations, routes, owner_map, damp_pct, scale_code, weight_panel):
    tok_dev, top_count, hidden_width = activations.shape
    experts = owner_map.shape[0]
    capacity = 2 * tok_dev * top_count // experts
    slot_ids, position = destinations(routes, owner_map)
    outbound = bucket(activations.reshape(-1, hidden_width), slot_ids * capacity + position, experts * capacity)
    outbound = outbound.reshape(experts, capacity, hidden_width)
    received = lax.all_to_all(outbound, ("expert", "help"), split_axis=0, concat_axis=0, tiled=True)
    strip, coeff, coeff_t = factor_strip(received.reshape(-1, hidden_width), damp_pct, tok_dev * top_count)
    levels = quantize(coeff, coeff_t, weight_panel[0], scale_code[0])
    return (levels[None], strip[None])


def solution(mesh):
    in_specs = (
        P(("expert", "help"), None, None),
        P(("expert", "help"), None),
        P(),
        P(("expert", "help")),
        P(("expert", "help"), None),
        P(("expert", "help"), None, None),
    )
    out_specs = (P(("expert", "help"), None, None), P(("expert", "help"), None, None))
    return jax.shard_map(shards, mesh=mesh, in_specs=in_specs, out_specs=out_specs, check_vma=False)
```
